128 devices in a mesh: section: 16 (over y_lo, x, core), dp: 8 (over y_hi, z).
Axes of the slice: x: 4, y: 4 (y_hi: 2, y_lo: 2; y = y_hi * 2 + y_lo), z: 4, core: 2. Of those that a mesh axis runs over, the one named last changes fastest.
Arguments:
- states: bfloat16 [2560, 3072], P(('section', 'dp')), may hold values from -6 to 6
- norm_gain: float32 [3072], replicated, may hold values from 0.1 to 1.9
- gate_weight: bfloat16 [3072, 12288], P(None, 'section'), may hold values from -0.109375 to 0.109375
- up_weight: bfloat16 [3072, 12288], P(None, 'section'), may hold values from -0.109375 to 0.109375
- down_weight: bfloat16 [12288, 3072], P('section'), may hold values from -0.0546875 to 0.0546875
- cotangent: bfloat16 [2560, 3072], P(('section', 'dp')), may hold values from -6 to 6
Outputs:
- final_states: bfloat16 [2560, 3072], P(('section', 'dp'))
- input_grads: float32 [2560, 3072], P(('section', 'dp'))
- gate_grads: float32 [3072, 12288], P('dp', 'section')
- up_grads: float32 [3072, 12288], P('dp', 'section')
- down_grads: float32 [12288, 3072], P('section', 'dp')
The draws below stay inside these ranges and needn't reach their ends.
All inputs are finite; a program needn't handle non-finite values.
Results may differ from the reference program's by a relative error of at most 0.029.
Values may be sent and summed in bfloat16 or wider, within the bound.
No kernel may reach another device: no remote copies, remote signals or barrier semaphores. Data moves between devices by JAX's collectives and lax.ppermute only.
A program may use at most 192 MiB of HBM per device.

```python
import jax
import jax.numpy as jnp
from jax import lax

D = 3072
FF = 12288
PASSES = 2
TOK_DEV = 20
TOKENS = 2560
N_SECTION = 16
N_DP = 8


def block_levels(rng, shape, shards, low, top_value):
    def one(position, parts):
        heights = jax.random.uniform(jax.random.fold_in(jax.random.fold_in(rng, 6), position), (parts,), jnp.float32, low / len(shards), top_value / len(shards))
        return jnp.repeat(jnp.exp(heights), shape[position] // parts).reshape((-1,) + (1,) * (len(shape) - position - 1))

    gain = one(*shards[0])
    for cut in shards[1:]:
        gain = gain * one(*cut)
    return gain


def bell_draw(own_key, dims, deviation, bound, shards=(), dtype=jnp.bfloat16):
    entries = jax.random.normal(own_key, dims, jnp.float32) * deviation
    if len(shards) > 0:
        entries = block_levels(own_key, dims, shards, -0.22, 0.18) * entries
    return jnp.clip(entries, min=-bound, max=bound).astype(dtype)


def setup_inputs(seed: int = 0) -> dict:
    seeds = jax.random.split(jax.random.key(seed), 7)
    return {
        "states": bell_draw(seeds[0], (TOKENS, D), 1.0, 6.0, ((0, 128),)),
        "norm_gain": jnp.clip(1.0 + 0.18 * jax.random.normal(seeds[1], (D,), jnp.float32), 0.1, 1.9),
        "gate_weight": bell_draw(seeds[2], (D, FF), D ** -0.5, 0.109375, ((1, 16),)),
        "up_weight": bell_draw(seeds[3], (D, FF), D ** -0.5, 0.109375, ((1, 16),)),
        "down_weight": bell_draw(seeds[4], (FF, D), FF ** -0.5, 0.0546875, ((0, 16),)),
        "cotangent": bell_draw(seeds[5], (TOKENS, D), 1.0, 6.0, ((0, 128),)),
    }


EPS = 1e-06

def normalize(values):
    widened = values.astype(jnp.float32)
    meansq = lax.optimization_barrier(jnp.mean(widened * widened, axis=-1, keepdims=True))
    inv_rms = lax.rsqrt(meansq + EPS)
    return (widened * inv_rms, inv_rms)

def norm_back(prev_rows, d_normed, norm_gain):
    x_hat, inv_rms = normalize(prev_rows)
    scaled = d_normed * norm_gain
    return inv_rms * (scaled - x_hat * lax.optimization_barrier(jnp.mean(scaled * x_hat, axis=-1, keepdims=True)))

def group_rows(values, group_index):
    width = values.shape[-1]
    blocks = values.reshape(N_SECTION, N_DP, TOK_DEV, width)
    return blocks[:, group_index].reshape(N_SECTION * TOK_DEV, width)

def reference(states, norm_gain, gate_weight, up_weight, down_weight, cotangent):
    hidden = states
    saved = []
    for pass_index in range(PASSES):
        x_hat, inv_rms = normalize(hidden)
        normed = (x_hat * norm_gain).astype(jnp.bfloat16)
        gate_pre = jnp.dot(normed, gate_weight, preferred_element_type=jnp.float32)
        up_pre = jnp.dot(normed, up_weight, preferred_element_type=jnp.float32)
        hidden_act = (jax.nn.silu(gate_pre) * up_pre).astype(jnp.bfloat16)
        block_out = jnp.dot(hidden_act, down_weight, preferred_element_type=jnp.float32)
        saved.append((hidden, normed, gate_pre, up_pre, hidden_act))
        hidden = (hidden.astype(jnp.float32) + block_out).astype(jnp.bfloat16)
    grad_state = cotangent.astype(jnp.float32)
    records = []
    for pass_index in reversed(range(PASSES)):
        prev_rows, normed, gate_pre, up_pre, hidden_act = saved[pass_index]
        grad_low = grad_state.astype(jnp.bfloat16)
        d_act = jnp.dot(grad_low, down_weight.T, preferred_element_type=jnp.float32)
        gate_sig = jax.nn.sigmoid(gate_pre)
        gate_low = (d_act * up_pre * gate_sig * (1.0 + gate_pre * (1.0 - gate_sig))).astype(jnp.bfloat16)
        up_low = (d_act * gate_pre * gate_sig).astype(jnp.bfloat16)
        d_normed = jnp.dot(gate_low, gate_weight.T, preferred_element_type=jnp.float32)
        d_normed = d_normed + jnp.dot(up_low, up_weight.T, preferred_element_type=jnp.float32)
        grad_state = grad_state + norm_back(prev_rows, d_normed, norm_gain)
        records.append((normed, hidden_act, grad_low, gate_low, up_low))
    gate_total = jnp.zeros((D, FF), jnp.float32)
    up_total = jnp.zeros((D, FF), jnp.float32)
    down_total = jnp.zeros((FF, D), jnp.float32)
    for group_index in range(N_DP):
        gate_part = jnp.zeros((D, FF), jnp.float32)
        up_part = jnp.zeros((D, FF), jnp.float32)
        down_part = jnp.zeros((FF, D), jnp.float32)
        for record in records:
            normed, hidden_act, grad_low, gate_low, up_low = [group_rows(item, group_index) for item in record]
            gate_part = gate_part + jnp.dot(normed.T, gate_low, preferred_element_type=jnp.float32)
            up_part = up_part + jnp.dot(normed.T, up_low, preferred_element_type=jnp.float32)
            down_part = down_part + jnp.dot(hidden_act.T, grad_low, preferred_element_type=jnp.float32)
        gate_total = gate_total + lax.optimization_barrier(gate_part.astype(jnp.bfloat16)).astype(jnp.float32)
        up_total = up_total + lax.optimization_barrier(up_part.astype(jnp.bfloat16)).astype(jnp.float32)
        down_total = down_total + lax.optimization_barrier(down_part.astype(jnp.bfloat16)).astype(jnp.float32)
    return (hidden, grad_state, gate_total, up_total, down_total)
```

```python
import jax
import jax.numpy as jnp
from jax import lax
from jax.sharding import PartitionSpec as P

EPS = 1e-06
N_Y, N_X, N_C = 2, 4, 2
N_H, N_Z = 2, 4
BF = jnp.bfloat16
F32 = jnp.float32


def section_move(values, dy, dx, dc):
    pairs = []
    for y in range(N_Y):
        for x in range(N_X):
            for c in range(N_C):
                source = (y * N_X + x) * N_C + c
                target = ((y + dy) % N_Y * N_X + (x + dx) % N_X) * N_C + (c + dc) % N_C
                pairs.append((source, target))
    return lax.ppermute(values, "section", pairs)


def dp_move(values, dh, dz):
    pairs = []
    for h in range(N_H):
        for z in range(N_Z):
            pairs.append((h * N_Z + z, (h + dh) % N_H * N_Z + (z + dz) % N_Z))
    return lax.ppermute(values, "dp", pairs)


def stacked(parts):
    return lax.optimization_barrier(jnp.concatenate(parts, axis=0))


def gather_rows(own):
    pair = stacked([own, section_move(own, 1, 0, 0)])
    arrivals = [section_move(pair, 0, -dx, 0) for dx in range(N_X)[1:]]
    line = stacked([pair] + arrivals)
    return stacked([line, section_move(line, 0, 0, 1)])


def scatter_rows(terms):
    half = terms.shape[0] // N_C
    line = terms[:half].astype(F32) + section_move(terms[half:], 0, 0, 1).astype(F32)
    line_low = line.astype(BF)
    quarter = half // N_X
    total = line[:quarter]
    for dx in range(N_X)[1:]:
        total = total + section_move(line_low[dx * quarter : (dx + 1) * quarter], 0, dx, 0).astype(F32)
    own = quarter // N_Y
    return total[:own] + section_move(total[own:].astype(BF), 1, 0, 0).astype(F32)


def normalize(values):
    widened = values.astype(F32)
    inv_rms = lax.rsqrt(jnp.mean(widened * widened, axis=-1, keepdims=True) + EPS)
    return (widened * inv_rms, inv_rms)


def norm_back(x_hat, inv_rms, d_normed, norm_gain):
    scaled = d_normed * norm_gain
    return inv_rms * (scaled - x_hat * jnp.mean(scaled * x_hat, axis=-1, keepdims=True))


def dot(left, right):
    return jnp.dot(left, right, preferred_element_type=F32)


def dot_t(left, right):
    return lax.dot_general(left, right, (((1,), (1,)), ((), ())), preferred_element_type=F32)


def dot_tokens(left, right):
    return lax.dot_general(left, right, (((0,), (0,)), ((), ())), preferred_element_type=F32)


def local(states, norm_gain, gate_weight, up_weight, down_weight, cotangent):
    width = states.shape[1]
    half = width // N_H
    block = half // N_Z
    me = lax.axis_index("dp")
    my_h, my_z = me // N_Z, me % N_Z

    def column_halves(values):
        mine = lax.dynamic_slice_in_dim(values, my_h * half, half, axis=1)
        others = lax.dynamic_slice_in_dim(values, (1 - my_h) * half, half, axis=1)
        return (mine, dp_move(others, 1, 0))

    def swap(values):
        return dp_move(values, 1, 0)

    def columns(values, dz):
        return lax.dynamic_slice_in_dim(values, (my_z + dz) % N_Z * block, block, axis=1)

    grad_cols, normed_cols, acts, gates, ups = {}, {}, {}, {}, {}

    def project(normed):
        gate_pre = dot(normed, gate_weight)
        up_pre = dot(normed, up_weight)
        sig = jax.nn.sigmoid(gate_pre)
        act = (gate_pre * sig * up_pre).astype(BF)
        to_gate = up_pre * sig * (1.0 + gate_pre * (1.0 - sig))
        to_up = gate_pre * sig
        return act, to_gate, to_up

    x0, inv0 = normalize(states)
    normed0 = gather_rows((x0 * norm_gain).astype(BF))
    grad1 = gather_rows(cotangent)
    act0, to_gate0, to_up0 = project(normed0)
    m0 = scatter_rows(dot(act0, down_weight).astype(BF))
    h1 = (states.astype(F32) + m0).astype(BF)

    x1, inv1 = normalize(h1)
    normed1 = gather_rows((x1 * norm_gain).astype(BF))
    act1, to_gate1, to_up1 = project(normed1)
    d_act1 = dot_t(grad1, down_weight)
    gate1 = (d_act1 * to_gate1).astype(BF)
    up1 = (d_act1 * to_up1).astype(BF)
    n1 = scatter_rows((dot_t(gate1, gate_weight) + dot_t(up1, up_weight)).astype(BF))
    r1 = cotangent.astype(F32) + norm_back(x1, inv1, n1, norm_gain)
    grad0 = gather_rows(r1.astype(BF))
    m1 = scatter_rows(dot(act1, down_weight).astype(BF))
    final_states = (h1.astype(F32) + m1).astype(BF)

    d_act0 = dot_t(grad0, down_weight)
    d_act0_swapped = swap(d_act0.astype(BF)).astype(F32)
    to_gate0_low, to_up0_low = to_gate0.astype(BF), to_up0.astype(BF)
    to_gate0_swapped, to_up0_swapped = swap(to_gate0_low), swap(to_up0_low)
    gate0 = (d_act0 * to_gate0).astype(BF)
    up0 = (d_act0 * to_up0).astype(BF)
    gate0_swapped = (d_act0_swapped * to_gate0_swapped.astype(F32)).astype(BF)
    up0_swapped = (d_act0_swapped * to_up0_swapped.astype(F32)).astype(BF)
    n0 = scatter_rows((dot_t(gate0, gate_weight) + dot_t(up0, up_weight)).astype(BF))
    input_grads = r1 + norm_back(x0, inv0, n0, norm_gain)

    normed0_cols, normed1_cols = column_halves(normed0), column_halves(normed1)
    grad1_cols, grad0_cols = column_halves(grad1), column_halves(grad0)
    act0_both, act1_both = (act0, swap(act0)), (act1, swap(act1))
    gate1_both, up1_both = (gate1, swap(gate1)), (up1, swap(up1))
    gate0_both, up0_both = (gate0, gate0_swapped), (up0, up0_swapped)

    def reduce_blocks(term):
        total = term(0)
        for dz in range(N_Z)[1:]:
            total = total + dp_move(term(dz).astype(BF), 0, dz).astype(F32)
        return total

    def in_term(first, second):
        def term(dz):
            parts = [
                dot_tokens(columns(cols, dz), rows)
                for both_cols, both_rows in ((normed1_cols, first), (normed0_cols, second))
                for cols, rows in zip(both_cols, both_rows)
            ]
            return (parts[0] + parts[1]) + (parts[2] + parts[3])

        return term

    def out_term(dz):
        parts = [
            dot_tokens(rows, columns(cols, dz))
            for both_cols, both_rows in ((grad1_cols, act1_both), (grad0_cols, act0_both))
            for cols, rows in zip(both_cols, both_rows)
        ]
        return (parts[0] + parts[1]) + (parts[2] + parts[3])

    gate_grads = reduce_blocks(in_term(gate1_both, gate0_both))
    up_grads = reduce_blocks(in_term(up1_both, up0_both))
    down_grads = reduce_blocks(out_term)
    return (final_states, input_grads, gate_grads, up_grads, down_grads)


def solution(mesh):
    in_specs = (
        P(("section", "dp"), None),
        P(),
        P(None, "section"),
        P(None, "section"),
        P("section", None),
        P(("section", "dp"), None),
    )
    out_specs = (
        P(("section", "dp"), None),
        P(("section", "dp"), None),
        P("dp", "section"),
        P("dp", "section"),
        P("section", "dp"),
    )
    return jax.shard_map(local, mesh=mesh, in_specs=in_specs, out_specs=out_specs, check_vma=False)
```

```python
import jax
import jax.numpy as jnp
from jax import lax
from jax.experimental import pallas as pl
from jax.experimental.pallas import tpu as pltpu
from jax.sharding import PartitionSpec as P

EPS = 1e-06
N_Y, N_X, N_C = 2, 4, 2
N_H, N_Z = 2, 4
BF = jnp.bfloat16
F32 = jnp.float32


def section_move(values, dy, dx, dc):
    pairs = []
    for y in range(N_Y):
        for x in range(N_X):
            for c in range(N_C):
                source = (y * N_X + x) * N_C + c
                target = ((y + dy) % N_Y * N_X + (x + dx) % N_X) * N_C + (c + dc) % N_C
                pairs.append((source, target))
    return lax.ppermute(values, "section", pairs)


def dp_move(values, target):
    pairs = []
    for h in range(N_H):
        for z in range(N_Z):
            to_h, to_z = target(h, z)
            pairs.append((h * N_Z + z, to_h % N_H * N_Z + to_z % N_Z))
    return lax.ppermute(values, "dp", pairs)


def over_h(values):
    return dp_move(values, lambda h, z: (h + 1, z))


def over_z(values):
    return dp_move(values, lambda h, z: (h, z + 2))


def after(values, *others):
    return lax.optimization_barrier((values,) + others)[0]


def stacked(parts):
    return lax.optimization_barrier(jnp.concatenate(parts, axis=0))


def gather_line(pair):
    blocks = {dx: section_move(pair, 0, -dx, 0) for dx in (2, 1, 3)}
    return stacked([pair] + [blocks[dx] for dx in range(N_X)[1:]])


def gather_core(line):
    return stacked([line, section_move(line, 0, 0, 1)])


def gather_pair(own):
    return stacked([own, section_move(own, 1, 0, 0)])


def scatter_core(terms):
    half = terms.shape[0] // N_C
    return terms[:half].astype(F32) + section_move(terms[half:], 0, 0, 1).astype(F32)


def scatter_line(line):
    line_low = line.astype(BF)
    quarter = line.shape[0] // N_X
    total = line[:quarter]
    for dx in (2, 1, 3):
        total = total + section_move(line_low[dx * quarter : (dx + 1) * quarter], 0, dx, 0).astype(F32)
    return total


def scatter_pair(total):
    own = total.shape[0] // N_Y
    return total[:own] + section_move(total[own:].astype(BF), 1, 0, 0).astype(F32)


def normalize(values):
    widened = values.astype(F32)
    inv_rms = lax.rsqrt(jnp.mean(widened * widened, axis=-1, keepdims=True) + EPS)
    return (widened * inv_rms, inv_rms)


def norm_back(x_hat, inv_rms, d_normed, norm_gain):
    scaled = d_normed * norm_gain
    return inv_rms * (scaled - x_hat * jnp.mean(scaled * x_hat, axis=-1, keepdims=True))


def dot(left, right):
    return jnp.dot(left, right, preferred_element_type=F32)


def dot_t(left, right):
    return lax.dot_general(left, right, (((1,), (1,)), ((), ())), preferred_element_type=F32)


def dot_tokens(left, right):
    return lax.dot_general(left, right, (((0,), (0,)), ((), ())), preferred_element_type=F32)


def in_kernel(*refs):
    cols, (d_other, gate_other, up_other), rows = refs[:4], refs[4:7], (refs[7:10], refs[10:13])
    out, grads = refs[13:]
    hidden = d_other.shape[1]
    parts = (pl.ds(0, hidden), pl.ds(hidden, hidden))

    @pl.when(pl.program_id(0) == 0)
    def _():
        d_wide = d_other[...].astype(F32)
        for part, factor in zip(parts, (gate_other, up_other)):
            grads[:, part] = (d_wide * factor[...].astype(F32)).astype(BF)

    for part, own in zip(parts, rows):
        total = dot_tokens(cols[0][...], own[0][...])
        for col, row in zip(cols[1:], own[1:]):
            total = total + dot_tokens(col[...], row[...])
        out[0, :, part] = (total + dot_tokens(cols[3][...], grads[:, part])).astype(out.dtype)


def column_specs(cols, block):
    return [
        pl.BlockSpec((values.shape[0], block), lambda i, first=first: (0, first + i))
        for values, first in cols
    ]


def whole_specs(rows):
    return [pl.BlockSpec(r.shape, lambda i: (0, 0)) for r in rows]


def in_products(cols, factors, gate_rows, up_rows, block, count, dtype):
    tokens, hidden = gate_rows[0].shape
    rows = factors + gate_rows + up_rows
    return pl.pallas_call(
        in_kernel,
        grid=(count,),
        in_specs=column_specs(cols, block) + whole_specs(rows),
        out_specs=pl.BlockSpec((1, block, 2 * hidden), lambda i: (i, 0, 0)),
        out_shape=jax.ShapeDtypeStruct((count, block, 2 * hidden), dtype),
        scratch_shapes=[pltpu.VMEM((tokens, 2 * hidden), BF)],
        compiler_params=pltpu.CompilerParams(vmem_limit_bytes=36 * 1024 * 1024),
        cost_estimate=pl.CostEstimate(
            flops=16 * count * tokens * block * hidden,
            bytes_accessed=18 * tokens * hidden + 8 * count * block * hidden,
            transcendentals=0,
        ),
    )(*[values for values, _ in cols], *rows)


def out_kernel(*refs):
    cols, rows, out = refs[:4], refs[4:8], refs[8]
    total = dot_tokens(rows[0][...], cols[0][...])
    for row, col in zip(rows[1:], cols[1:]):
        total = total + dot_tokens(row[...], col[...])
    out[0] = total


def out_products(cols, rows, block, count):
    tokens, hidden = rows[0].shape
    return pl.pallas_call(
        out_kernel,
        grid=(count,),
        in_specs=column_specs(cols, block) + whole_specs(rows),
        out_specs=pl.BlockSpec((1, hidden, block), lambda i: (i, 0, 0)),
        out_shape=jax.ShapeDtypeStruct((count, hidden, block), F32),
        compiler_params=pltpu.CompilerParams(vmem_limit_bytes=36 * 1024 * 1024),
        cost_estimate=pl.CostEstimate(
            flops=8 * count * tokens * block * hidden,
            bytes_accessed=16 * tokens * hidden + 4 * count * block * hidden,
            transcendentals=0,
        ),
    )(*[values for values, _ in cols], *rows)


def local(states, norm_gain, gate_weight, up_weight, down_weight, cotangent):
    width = states.shape[1]
    block = width // (N_H * N_Z)
    me = lax.axis_index("dp")
    my_h, my_z = me // N_Z, me % N_Z
    side = my_z // 2

    def columns(values, numbers):
        parts = [lax.dynamic_slice_in_dim(values, n * block, block, axis=1) for n in numbers]
        return jnp.concatenate(parts, axis=1)

    def of_h(values, h, distances):
        return columns(values, [h * N_Z + (my_z + dz) % N_Z for dz in distances])

    def of_side(values, s, distances):
        return columns(
            values,
            [
                (my_h + dh) % N_H * N_Z + s * 2 + (my_z + dz) % 2
                for dh in distances
                for dz in range(2)
            ],
        )

    def project(normed):
        gate_pre = dot(normed, gate_weight)
        up_pre = dot(normed, up_weight)
        sig = jax.nn.sigmoid(gate_pre)
        act = (gate_pre * sig * up_pre).astype(BF)
        to_gate = up_pre * sig * (1.0 + gate_pre * (1.0 - sig))
        to_up = gate_pre * sig
        return act, to_gate, to_up

    x0, inv0 = normalize(states)
    pair0 = gather_pair((x0 * norm_gain).astype(BF))
    line0 = gather_line(pair0)
    cot_pair = gather_pair(after(cotangent, pair0))
    normed0 = gather_core(after(line0, cot_pair))
    act0, to_gate0, to_up0 = project(normed0)
    to_gate0_other = over_z(to_gate0.astype(BF))
    term0 = dot(act0, down_weight).astype(BF)
    core0 = after(scatter_core(term0), to_gate0_other)
    to_up0_other = over_z(after(to_up0.astype(BF), to_gate0_other))
    act0_other = over_h(after(act0, term0))
    total0 = after(scatter_line(core0), to_up0_other, act0_other)
    cot_line = gather_line(after(cot_pair, total0))
    normed0_near = over_z(after(of_side(normed0, 1 - side, (0,)), total0))
    h1 = (states.astype(F32) + scatter_pair(total0)).astype(BF)

    x1, inv1 = normalize(h1)
    pair1 = after(gather_pair((x1 * norm_gain).astype(BF)), cot_line, normed0_near)
    normed0_far = over_z(after(of_side(normed0, 1 - side, (1,)), pair1))
    grad1 = gather_core(after(cot_line, pair1))
    grad1_near = over_h(of_h(grad1, 1 - my_h, (0, 1)))
    normed1 = gather_core(after(gather_line(pair1), grad1_near, normed0_far))
    act1, to_gate1, to_up1 = project(normed1)
    d_act1 = dot_t(grad1, down_weight)
    gate1 = (d_act1 * to_gate1).astype(BF)
    up1 = (d_act1 * to_up1).astype(BF)
    gate1_other = over_z(gate1)
    term1 = (dot_t(gate1, gate_weight) + dot_t(up1, up_weight)).astype(BF)
    core1 = after(scatter_core(term1), gate1_other)
    up1_other = over_z(after(up1, gate1_other))
    grad1_far = over_h(after(of_h(grad1, 1 - my_h, (2, 3)), term1))
    total1 = after(scatter_line(core1), up1_other, grad1_far)
    core_m1 = scatter_core(after(dot(act1, down_weight).astype(BF), term1))
    total_m1 = scatter_line(after(core_m1, total1))
    normed1_near = over_z(after(of_side(normed1, 1 - side, (0,)), total1))
    r1 = cotangent.astype(F32) + norm_back(x1, inv1, scatter_pair(total1), norm_gain)
    pair2 = after(gather_pair(r1.astype(BF)), total_m1, normed1_near)
    normed1_far = over_z(after(of_side(normed1, 1 - side, (1,)), pair2))
    act1_other = over_h(after(act1, pair2))
    line2 = after(gather_line(pair2), normed1_far, act1_other)
    final_states = (h1.astype(F32) + scatter_pair(after(total_m1, line2))).astype(BF)
    grad0 = gather_core(line2)

    d_act0 = dot_t(grad0, down_weight)
    d_act0_other = over_z(d_act0.astype(BF))
    grad0_other = over_h(of_h(grad0, 1 - my_h, range(N_Z)))
    gate0 = (d_act0 * to_gate0).astype(BF)
    up0 = (d_act0 * to_up0).astype(BF)
    term2 = (dot_t(gate0, gate_weight) + dot_t(up0, up_weight)).astype(BF)
    core2 = after(scatter_core(term2), d_act0_other)
    n0 = scatter_pair(scatter_line(core2))
    input_grads = r1 + norm_back(x0, inv0, n0, norm_gain)

    normed1_own, normed0_own = of_side(normed1, side, (0, 1)), of_side(normed0, side, (0, 1))
    factors = (d_act0_other, to_gate0_other, to_up0_other)

    def in_term(first, count, dtype):
        if first < 2:
            others = ((normed1_near, first), (normed0_near, first))
        else:
            others = ((normed1_far, first - 2), (normed0_far, first - 2))
        cols = ((normed1_own, first), others[0], (normed0_own, first), others[1])
        gate_rows, up_rows = (gate1, gate1_other, gate0), (up1, up1_other, up0)
        return in_products(cols, factors, gate_rows, up_rows, block, count, dtype)

    def out_term(first, grad1_part):
        cols = ((grad1_own, first), (grad1_part, 0), (grad0_own, first), (late_other, first))
        return out_products(cols, (act1, act1_other, act0, act0_other), block, 2)

    def over_y(values):
        return dp_move(values, lambda h, z: (h + 1, z)).astype(F32)

    def over_link(values):
        return dp_move(values, lambda h, z: (h, z + 1 - 2 * (z % 2))).astype(F32)

    hidden = gate_weight.shape[1]
    far = in_term(3, 1, BF)[0]
    far_gate, far_up = over_y(far[:, :hidden]), over_link(far[:, hidden:])
    in_y = in_term(2, 1, F32)[0]
    gate_y = over_y(in_y[:, :hidden].astype(BF))
    near = in_term(0, 2, F32)
    own, in_z = near[0], near[1]
    up_z = over_link(in_z[:, hidden:].astype(BF))
    up_y = over_y((in_y[:, hidden:] + far_up).astype(BF))
    gate_z = over_link((in_z[:, :hidden] + far_gate).astype(BF))
    gate_grads = own[:, :hidden] + gate_y + gate_z
    up_grads = own[:, hidden:] + up_y + up_z
    grad1_own, grad0_own = of_h(grad1, my_h, range(N_Z)), of_h(grad0, my_h, range(N_Z))
    late_other = after(grad0_other, near)
    down23, down01 = out_term(2, grad1_far), out_term(0, grad1_near)
    down_grads = down01[0]
    for dz, term in ((2, down23[0]), (1, down01[1]), (3, down23[1])):
        term = after(term.astype(BF), far_gate, far_up)
        down_grads = down_grads + dp_move(term, lambda h, z, dz=dz: (h, z + dz)).astype(F32)
    return (final_states, input_grads, gate_grads, up_grads, down_grads)


def solution(mesh):
    in_specs = (
        P(("section", "dp"), None),
        P(),
        P(None, "section"),
        P(None, "section"),
        P("section", None),
        P(("section", "dp"), None),
    )
    out_specs = (
        P(("section", "dp"), None),
        P(("section", "dp"), None),
        P("dp", "section"),
        P("dp", "section"),
        P("section", "dp"),
    )
    return jax.shard_map(local, mesh=mesh, in_specs=in_specs, out_specs=out_specs, check_vma=False)
```

```python
import jax
import jax.numpy as jnp
from jax import lax
from jax.experimental import pallas as pl
from jax.experimental.pallas import tpu as pltpu
from jax.sharding import PartitionSpec as P

EPS = 1e-06
N_Y, N_X, N_C = 2, 4, 2
N_H, N_Z = 2, 4
BF = jnp.bfloat16
F32 = jnp.float32


def section_move(values, dy, dx, dc):
    pairs = []
    for y in range(N_Y):
        for x in range(N_X):
            for c in range(N_C):
                source = (y * N_X + x) * N_C + c
                target = ((y + dy) % N_Y * N_X + (x + dx) % N_X) * N_C + (c + dc) % N_C
                pairs.append((source, target))
    return lax.ppermute(values, "section", pairs)


def dp_move(values, target):
    pairs = []
    for h in range(N_H):
        for z in range(N_Z):
            to_h, to_z = target(h, z)
            pairs.append((h * N_Z + z, to_h % N_H * N_Z + to_z % N_Z))
    return lax.ppermute(values, "dp", pairs)


def over_h(values):
    return dp_move(values, lambda h, z: (h + 1, z))


def over_z(values):
    return dp_move(values, lambda h, z: (h, z + 2))


def after(values, *others):
    return lax.optimization_barrier((values,) + others)[0]


def stacked(parts):
    return lax.optimization_barrier(jnp.concatenate(parts, axis=0))


def gather_line(pair, *ready):
    first, second, third = (section_move(pair, 0, -dx, 0) for dx in range(N_X)[1:])
    first = after(first, *ready)
    return stacked([pair, first, after(second, first), after(third, first)])


def gather_core(line):
    return stacked([line, section_move(line, 0, 0, 1)])


def gather_pair(own):
    return stacked([own, section_move(own, 1, 0, 0)])


def scatter_core(terms):
    half = terms.shape[0] // N_C
    return terms[:half].astype(F32) + section_move(terms[half:], 0, 0, 1).astype(F32)


def scatter_line(line, *ready):
    line_low = line.astype(BF)
    quarter = line.shape[0] // N_X
    first, second, third = (
        section_move(line_low[dx * quarter : (dx + 1) * quarter], 0, dx, 0).astype(F32)
        for dx in range(N_X)[1:]
    )
    total = after(line[:quarter] + first, *ready)
    return total + after(second, total) + after(third, total)


def scatter_far(line):
    half = line.shape[0] // 2
    return line[:half] + section_move(line[half:].astype(BF), 0, 2, 0).astype(F32)


def scatter_near(line):
    quarter = line.shape[0] // 2
    return line[:quarter] + section_move(line[quarter:].astype(BF), 0, 1, 0).astype(F32)


def scatter_pair(total):
    own = total.shape[0] // N_Y
    return total[:own] + section_move(total[own:].astype(BF), 1, 0, 0).astype(F32)


def normalize(values):
    widened = values.astype(F32)
    inv_rms = lax.rsqrt(jnp.mean(widened * widened, axis=-1, keepdims=True) + EPS)
    return (widened * inv_rms, inv_rms)


def norm_back(x_hat, inv_rms, d_normed, norm_gain):
    scaled = d_normed * norm_gain
    return inv_rms * (scaled - x_hat * jnp.mean(scaled * x_hat, axis=-1, keepdims=True))


def dot(left, right):
    return jnp.dot(left, right, preferred_element_type=F32)


def dot_t(left, right):
    return lax.dot_general(left, right, (((1,), (1,)), ((), ())), preferred_element_type=F32)


def dot_tokens(left, right):
    return lax.dot_general(left, right, (((0,), (0,)), ((), ())), preferred_element_type=F32)


def in_kernel(*refs):
    cols, (d_other, gate_other, up_other), rows = refs[:4], refs[4:7], (refs[7:10], refs[10:13])
    out, grads = refs[13:]
    hidden = d_other.shape[1]
    parts = (pl.ds(0, hidden), pl.ds(hidden, hidden))

    @pl.when(pl.program_id(0) == 0)
    def _():
        d_wide = d_other[...].astype(F32)
        for part, factor in zip(parts, (gate_other, up_other)):
            grads[:, part] = (d_wide * factor[...].astype(F32)).astype(BF)

    for part, own in zip(parts, rows):
        total = dot_tokens(cols[0][...], own[0][...])
        for col, row in zip(cols[1:], own[1:]):
            total = total + dot_tokens(col[...], row[...])
        out[0, :, part] = (total + dot_tokens(cols[3][...], grads[:, part])).astype(out.dtype)


def column_specs(cols, block, first):
    return [pl.BlockSpec((c.shape[0], block), lambda i: (0, first + i)) for c in cols]


def whole_specs(rows):
    return [pl.BlockSpec(r.shape, lambda i: (0, 0)) for r in rows]


def in_products(cols, factors, gate_rows, up_rows, block, first, count, dtype):
    tokens, hidden = gate_rows[0].shape
    rows = factors + gate_rows + up_rows
    return pl.pallas_call(
        in_kernel,
        grid=(count,),
        in_specs=column_specs(cols, block, first) + whole_specs(rows),
        out_specs=pl.BlockSpec((1, block, 2 * hidden), lambda i: (i, 0, 0)),
        out_shape=jax.ShapeDtypeStruct((count, block, 2 * hidden), dtype),
        scratch_shapes=[pltpu.VMEM((tokens, 2 * hidden), BF)],
        compiler_params=pltpu.CompilerParams(vmem_limit_bytes=36 * 1024 * 1024),
        cost_estimate=pl.CostEstimate(
            flops=16 * count * tokens * block * hidden,
            bytes_accessed=18 * tokens * hidden + 8 * count * block * hidden,
            transcendentals=0,
        ),
    )(*cols, *rows)


def out_kernel(*refs):
    cols, rows, out = refs[:4], refs[4:8], refs[8]
    total = dot_tokens(rows[0][...], cols[0][...])
    for row, col in zip(rows[1:], cols[1:]):
        total = total + dot_tokens(row[...], col[...])
    out[0] = total


def out_products(cols, rows, block, first, count):
    tokens, hidden = rows[0].shape
    return pl.pallas_call(
        out_kernel,
        grid=(count,),
        in_specs=column_specs(cols, block, first) + whole_specs(rows),
        out_specs=pl.BlockSpec((1, hidden, block), lambda i: (i, 0, 0)),
        out_shape=jax.ShapeDtypeStruct((count, hidden, block), F32),
        compiler_params=pltpu.CompilerParams(vmem_limit_bytes=36 * 1024 * 1024),
        cost_estimate=pl.CostEstimate(
            flops=8 * count * tokens * block * hidden,
            bytes_accessed=16 * tokens * hidden + 4 * count * block * hidden,
            transcendentals=0,
        ),
    )(*cols, *rows)


def local(states, norm_gain, gate_weight, up_weight, down_weight, cotangent):
    width = states.shape[1]
    block = width // (N_H * N_Z)
    me = lax.axis_index("dp")
    my_h, my_z = me // N_Z, me % N_Z
    side = my_z // 2

    def columns(values, numbers):
        parts = [lax.dynamic_slice_in_dim(values, n * block, block, axis=1) for n in numbers]
        return jnp.concatenate(parts, axis=1)

    def of_h(values, h):
        return columns(values, [h * N_Z + (my_z + dz) % N_Z for dz in (1, 3, 2, 0)])

    def of_side(values, s):
        return columns(
            values,
            [
                (my_h + dh) % N_H * N_Z + s * 2 + (my_z + dz) % 2
                for dh in range(N_H)
                for dz in range(2)
            ],
        )

    def project(normed):
        gate_pre = dot(normed, gate_weight)
        up_pre = dot(normed, up_weight)
        sig = jax.nn.sigmoid(gate_pre)
        act = (gate_pre * sig * up_pre).astype(BF)
        to_gate = up_pre * sig * (1.0 + gate_pre * (1.0 - sig))
        to_up = gate_pre * sig
        return act, to_gate, to_up

    x0, inv0 = normalize(states)
    pair0 = gather_pair((x0 * norm_gain).astype(BF))
    line0 = gather_line(pair0)
    cot_pair = gather_pair(after(cotangent, pair0))
    normed0 = gather_core(after(line0, cot_pair))
    act0, to_gate0, to_up0 = project(normed0)
    term0 = dot(act0, down_weight).astype(BF)
    normed0_half = over_z(after(of_side(line0, 1 - side), term0))
    act0_other = over_h(after(act0, term0))
    total0 = scatter_line(scatter_core(term0), normed0_half, act0_other)
    cot_line = gather_line(after(cot_pair, total0))
    to_gate0_other = over_z(after(to_gate0.astype(BF), total0))
    h1 = (states.astype(F32) + scatter_pair(total0)).astype(BF)

    x1, inv1 = normalize(h1)
    pair1 = after(gather_pair((x1 * norm_gain).astype(BF)), cot_line, to_gate0_other)
    to_up0_other = over_z(after(to_up0.astype(BF), to_gate0_other))
    grad1_half = over_h(after(of_h(cot_line, 1 - my_h), pair1))
    line1 = gather_line(pair1, to_up0_other, grad1_half)
    grad1 = gather_core(after(cot_line, pair1))
    normed1 = gather_core(after(line1, grad1))
    normed0_other = gather_core(after(normed0_half, normed1))
    act1, to_gate1, to_up1 = project(normed1)
    d_act1 = dot_t(grad1, down_weight)
    gate1 = (d_act1 * to_gate1).astype(BF)
    up1 = (d_act1 * to_up1).astype(BF)
    term1 = (dot_t(gate1, gate_weight) + dot_t(up1, up_weight)).astype(BF)
    gate1_other = over_z(after(gate1, term1))
    act1_other = over_h(after(act1, term1))
    core1 = scatter_core(term1)
    term_m1 = dot(after(act1, core1), down_weight).astype(BF)
    total1 = scatter_line(core1, gate1_other, act1_other, term_m1)
    up1_other = over_z(after(up1, total1))
    core_m1 = scatter_core(after(term_m1, total1))
    r1 = cotangent.astype(F32) + norm_back(x1, inv1, scatter_pair(total1), norm_gain)
    pair2 = after(gather_pair(r1.astype(BF)), up1_other)
    normed1_half = over_z(after(of_side(line1, 1 - side), up1_other))
    grad1_other = gather_core(after(grad1_half, pair2))
    line2 = after(gather_line(pair2, normed1_half), grad1_other, normed0_other, core_m1)
    grad0_half = over_h(of_h(line2, 1 - my_h))
    grad0 = gather_core(line2)

    d_act0 = dot_t(grad0, down_weight)
    d_act0_other = over_z(d_act0.astype(BF))
    normed1_other = gather_core(after(normed1_half, d_act0))
    gate0 = (d_act0 * to_gate0).astype(BF)
    up0 = (d_act0 * to_up0).astype(BF)

    term2 = (dot_t(gate0, gate_weight) + dot_t(up0, up_weight)).astype(BF)
    grad0_other = gather_core(after(grad0_half, term2))
    far_m1 = scatter_far(after(core_m1, term2))

    normed1_own, normed0_own = of_side(normed1, side), of_side(normed0, side)
    grad1_own, grad0_own = of_h(grad1, my_h), of_h(grad0, my_h)
    out_cols = (grad1_own, grad1_other, grad0_own, grad0_other)
    in_cols = (normed1_own, normed1_other, normed0_own, normed0_other)
    factors = (after(d_act0_other, term2), to_gate0_other, to_up0_other)

    def in_term(first, count, dtype, *ready):
        gate_rows, up_rows = (gate1, gate1_other, gate0), (up1, up1_other, up0)
        late = (after(factors[0], *ready),) + factors[1:]
        return in_products(in_cols, late, gate_rows, up_rows, block, first, count, dtype)

    def over_y(values):
        return dp_move(values, lambda h, z: (h + 1, z)).astype(F32)

    def over_link(values):
        return dp_move(values, lambda h, z: (h, z + 1 - 2 * (z % 2))).astype(F32)

    hidden = gate_weight.shape[1]
    def out_term(first, ready):
        return out_products(out_cols, (after(act1, ready), act1_other, act0, act0_other), block, first, 2)

    def down_move(term, dz, *ready):
        return dp_move(after(term.astype(BF), *ready), lambda h, z: (h, z + dz)).astype(F32)

    far = in_term(3, 1, BF)[0]
    far_sum = over_y(far)
    down13 = out_term(0, far)
    one, three = down_move(down13[0], 1), down_move(down13[1], 3)
    down20 = out_term(2, down13)
    core2 = scatter_core(after(term2, far))
    near = in_term(0, 3, F32, down20, core2, far_m1)
    own, in_z, in_y = near[0], near[1], near[2]
    two = down_move(down20[0], 2, one, three)
    far_n0 = scatter_far(core2)
    near_m1 = scatter_near(after(far_m1, far))
    far_sum = after(far_sum, two, far_n0, near_m1)
    from_y = over_y(after(in_y.astype(BF), far_sum))
    from_z = over_link((in_z + far_sum).astype(BF))
    m1 = scatter_pair(after(near_m1, far_sum))
    total2 = scatter_near(after(far_n0, far_sum))
    down_grads = down20[1] + one + two + three
    in_grads = own + from_y + from_z
    input_grads = r1 + norm_back(x0, inv0, scatter_pair(total2), norm_gain)
    final_states = (h1.astype(F32) + m1).astype(BF)
    return (final_states, input_grads, in_grads[:, :hidden], in_grads[:, hidden:], down_grads)


def solution(mesh):
    in_specs = (
        P(("section", "dp"), None),
        P(),
        P(None, "section"),
        P(None, "section"),
        P("section", None),
        P(("section", "dp"), None),
    )
    out_specs = (
        P(("section", "dp"), None),
        P(("section", "dp"), None),
        P("dp", "section"),
        P("dp", "section"),
        P("section", "dp"),
    )
    return jax.shard_map(local, mesh=mesh, in_specs=in_specs, out_specs=out_specs, check_vma=False)
```

```python
import jax
import jax.numpy as jnp
from jax import lax
from jax.experimental import pallas as pl
from jax.experimental.pallas import tpu as pltpu
from jax.sharding import PartitionSpec as P

EPS = 1e-06
N_Y, N_X, N_C = 2, 4, 2
N_H, N_Z = 2, 4
BF = jnp.bfloat16
F32 = jnp.float32


def section_move(values, dy, dx, dc):
    pairs = []
    for y in range(N_Y):
        for x in range(N_X):
            for c in range(N_C):
                source = (y * N_X + x) * N_C + c
                target = ((y + dy) % N_Y * N_X + (x + dx) % N_X) * N_C + (c + dc) % N_C
                pairs.append((source, target))
    return lax.ppermute(values, "section", pairs)


def dp_move(values, target):
    pairs = []
    for h in range(N_H):
        for z in range(N_Z):
            to_h, to_z = target(h, z)
            pairs.append((h * N_Z + z, to_h % N_H * N_Z + to_z % N_Z))
    return lax.ppermute(values, "dp", pairs)


def over_h(values):
    return dp_move(values, lambda h, z: (h + 1, z))


def over_z(values):
    return dp_move(values, lambda h, z: (h, z + 2))


def after(values, *others):
    return lax.optimization_barrier((values,) + others)[0]


def stacked(parts):
    return lax.optimization_barrier(jnp.concatenate(parts, axis=0))


def gather_line(pair, *ready):
    first, second, third = (section_move(pair, 0, -dx, 0) for dx in range(N_X)[1:])
    first = after(first, *ready)
    return stacked([pair, first, after(second, first), after(third, first)])


def gather_near(pair):
    return stacked([pair, section_move(pair, 0, -1, 0)])


def gather_far(near):
    return stacked([near, section_move(near, 0, -2, 0)])


def gather_core(line):
    return stacked([line, section_move(line, 0, 0, 1)])


def gather_pair(own):
    return stacked([own, section_move(own, 1, 0, 0)])


def scatter_core(terms):
    half = terms.shape[0] // N_C
    return terms[:half].astype(F32) + section_move(terms[half:], 0, 0, 1).astype(F32)


def scatter_line(line, *ready):
    line_low = line.astype(BF)
    quarter = line.shape[0] // N_X
    first, second, third = (
        section_move(line_low[dx * quarter : (dx + 1) * quarter], 0, dx, 0).astype(F32)
        for dx in range(N_X)[1:]
    )
    total = after(line[:quarter] + first, *ready)
    return total + after(second, total) + after(third, total)


def scatter_far(line):
    half = line.shape[0] // 2
    return line[:half] + section_move(line[half:].astype(BF), 0, 2, 0).astype(F32)


def scatter_near(line):
    quarter = line.shape[0] // 2
    return line[:quarter] + section_move(line[quarter:].astype(BF), 0, 1, 0).astype(F32)


def scatter_pair(total):
    own = total.shape[0] // N_Y
    return total[:own] + section_move(total[own:].astype(BF), 1, 0, 0).astype(F32)


def normalize(values):
    widened = values.astype(F32)
    inv_rms = lax.rsqrt(jnp.mean(widened * widened, axis=-1, keepdims=True) + EPS)
    return (widened * inv_rms, inv_rms)


def norm_back(x_hat, inv_rms, d_normed, norm_gain):
    scaled = d_normed * norm_gain
    return inv_rms * (scaled - x_hat * jnp.mean(scaled * x_hat, axis=-1, keepdims=True))


def dot(left, right):
    return jnp.dot(left, right, preferred_element_type=F32)


def dot_t(left, right):
    return lax.dot_general(left, right, (((1,), (1,)), ((), ())), preferred_element_type=F32)


def dot_tokens(left, right):
    return lax.dot_general(left, right, (((0,), (0,)), ((), ())), preferred_element_type=F32)


def in_kernel(*refs):
    cols, (d_other, gate_other, up_other), rows = refs[:4], refs[4:7], (refs[7:10], refs[10:13])
    out, grads = refs[13:]
    hidden = d_other.shape[1]
    parts = (pl.ds(0, hidden), pl.ds(hidden, hidden))

    @pl.when(pl.program_id(0) == 0)
    def _():
        d_wide = d_other[...].astype(F32)
        for part, factor in zip(parts, (gate_other, up_other)):
            grads[:, part] = (d_wide * factor[...].astype(F32)).astype(BF)

    for part, own in zip(parts, rows):
        total = dot_tokens(cols[0][...], own[0][...])
        for col, row in zip(cols[1:], own[1:]):
            total = total + dot_tokens(col[...], row[...])
        out[0, :, part] = (total + dot_tokens(cols[3][...], grads[:, part])).astype(out.dtype)


def column_specs(cols, block, first):
    return [pl.BlockSpec((c.shape[0], block), lambda i: (0, first + i)) for c in cols]


def row_specs(rows, hidden):
    return [pl.BlockSpec((r.shape[0], hidden), lambda i, part=part: (0, part)) for r, part in rows]


def in_products(cols, factors, gate_rows, up_rows, block, first, count, dtype):
    tokens, hidden = factors[0][0].shape
    rows = factors + gate_rows + up_rows
    return pl.pallas_call(
        in_kernel,
        grid=(count,),
        in_specs=column_specs(cols, block, first) + row_specs(rows, hidden),
        out_specs=pl.BlockSpec((1, block, 2 * hidden), lambda i: (i, 0, 0)),
        out_shape=jax.ShapeDtypeStruct((count, block, 2 * hidden), dtype),
        scratch_shapes=[pltpu.VMEM((tokens, 2 * hidden), BF)],
        compiler_params=pltpu.CompilerParams(vmem_limit_bytes=36 * 1024 * 1024),
        cost_estimate=pl.CostEstimate(
            flops=16 * count * tokens * block * hidden,
            bytes_accessed=18 * tokens * hidden + 8 * count * block * hidden,
            transcendentals=0,
        ),
    )(*cols, *(r for r, _ in rows))


def out_kernel(*refs):
    cols, rows, out = refs[:4], refs[4:8], refs[8]
    total = dot_tokens(rows[0][...], cols[0][...])
    for row, col in zip(rows[1:], cols[1:]):
        total = total + dot_tokens(row[...], col[...])
    out[0] = total


def out_products(cols, rows, block, first, count):
    tokens, hidden = rows[0].shape
    return pl.pallas_call(
        out_kernel,
        grid=(count,),
        in_specs=column_specs(cols, block, first) + row_specs([(r, 0) for r in rows], hidden),
        out_specs=pl.BlockSpec((1, hidden, block), lambda i: (i, 0, 0)),
        out_shape=jax.ShapeDtypeStruct((count, hidden, block), F32),
        compiler_params=pltpu.CompilerParams(vmem_limit_bytes=36 * 1024 * 1024),
        cost_estimate=pl.CostEstimate(
            flops=8 * count * tokens * block * hidden,
            bytes_accessed=16 * tokens * hidden + 4 * count * block * hidden,
            transcendentals=0,
        ),
    )(*cols, *rows)


def local(states, norm_gain, gate_weight, up_weight, down_weight, cotangent):
    width = states.shape[1]
    block = width // (N_H * N_Z)
    me = lax.axis_index("dp")
    my_h, my_z = me // N_Z, me % N_Z
    side = my_z // 2

    def columns(values, numbers):
        parts = [lax.dynamic_slice_in_dim(values, n * block, block, axis=1) for n in numbers]
        return jnp.concatenate(parts, axis=1)

    def of_h(values, h):
        return columns(values, [h * N_Z + (my_z + dz) % N_Z for dz in (1, 3, 2, 0)])

    def of_side(values, s):
        return columns(
            values,
            [
                (my_h + dh) % N_H * N_Z + s * 2 + (my_z + dz) % 2
                for dh in range(N_H)
                for dz in range(2)
            ],
        )

    def project(normed):
        gate_pre = dot(normed, gate_weight)
        up_pre = dot(normed, up_weight)
        sig = jax.nn.sigmoid(gate_pre)
        act = (gate_pre * sig * up_pre).astype(BF)
        to_gate = up_pre * sig * (1.0 + gate_pre * (1.0 - sig))
        to_up = gate_pre * sig
        return act, to_gate, to_up

    x0, inv0 = normalize(states)
    pair0 = gather_pair((x0 * norm_gain).astype(BF))
    line0 = gather_line(pair0)
    cot_pair = gather_pair(after(cotangent, pair0))
    normed0 = gather_core(after(line0, cot_pair))
    cot_near = gather_near(after(cot_pair, line0))
    act0, to_gate0, to_up0 = project(normed0)
    both0 = jnp.concatenate([to_gate0.astype(BF), to_up0.astype(BF)], axis=1)
    core0 = after(scatter_core(dot(act0, down_weight).astype(BF)), cot_near)
    normed0_half = over_z(after(of_side(line0, 1 - side), core0))
    total0 = scatter_line(core0, normed0_half)
    cot_line = gather_far(after(cot_near, total0))
    both0_other = over_z(after(both0, total0))
    h1 = (states.astype(F32) + scatter_pair(total0)).astype(BF)

    x1, inv1 = normalize(h1)
    pair1 = after(gather_pair((x1 * norm_gain).astype(BF)), cot_line)
    grad1_half = over_h(after(of_h(cot_line, 1 - my_h), pair1))
    line1 = gather_line(pair1, both0_other, grad1_half)
    grad1 = gather_core(after(cot_line, pair1))
    normed1 = gather_core(after(line1, grad1))
    normed0_other = gather_core(after(normed0_half, normed1))
    act1, to_gate1, to_up1 = project(normed1)
    d_act1 = dot_t(grad1, down_weight)
    gate1 = (d_act1 * to_gate1).astype(BF)
    up1 = (d_act1 * to_up1).astype(BF)
    term1 = (dot_t(gate1, gate_weight) + dot_t(up1, up_weight)).astype(BF)
    core1 = scatter_core(term1)
    normed1_half = over_z(after(of_side(line1, 1 - side), term1))
    act0_other = over_h(after(act0, term1))
    term_m1 = dot(after(act1, core1), down_weight).astype(BF)
    total1 = scatter_line(core1, normed1_half, act0_other, term_m1)
    gate1_other = over_z(after(gate1, total1))
    core_m1 = scatter_core(after(term_m1, total1))
    r1 = cotangent.astype(F32) + norm_back(x1, inv1, scatter_pair(total1), norm_gain)
    pair2 = after(gather_pair(r1.astype(BF)), core_m1, gate1_other)
    up1_other = over_z(after(up1, gate1_other))
    act1_other = over_h(after(act1, pair2))
    grad1_other = gather_core(after(grad1_half, pair2))
    line2 = after(gather_line(pair2, up1_other, act1_other), grad1_other, normed0_other)
    grad0_half = over_h(of_h(line2, 1 - my_h))
    grad0 = gather_core(line2)

    d_act0 = dot_t(grad0, down_weight)
    d_act0_other = over_z(d_act0.astype(BF))
    normed1_other = gather_core(after(normed1_half, d_act0))
    gate0 = (d_act0 * to_gate0).astype(BF)
    up0 = (d_act0 * to_up0).astype(BF)
    term2 = (dot_t(gate0, gate_weight) + dot_t(up0, up_weight)).astype(BF)
    grad0_other = gather_core(after(grad0_half, term2))
    far_m1 = scatter_far(after(core_m1, term2))

    normed1_own, normed0_own = of_side(normed1, side), of_side(normed0, side)
    grad1_own, grad0_own = of_h(grad1, my_h), of_h(grad0, my_h)
    out_cols = (grad1_own, grad1_other, grad0_own, grad0_other)
    in_cols = (normed1_own, normed1_other, normed0_own, normed0_other)

    def in_term(first, count, dtype, *ready):
        factors = ((after(d_act0_other, term2, *ready), 0), (both0_other, 0), (both0_other, 1))
        gate_rows = ((gate1, 0), (gate1_other, 0), (gate0, 0))
        up_rows = ((up1, 0), (up1_other, 0), (up0, 0))
        return in_products(in_cols, factors, gate_rows, up_rows, block, first, count, dtype)

    def over_y(values):
        return dp_move(values, lambda h, z: (h + 1, z)).astype(F32)

    def over_link(values):
        return dp_move(values, lambda h, z: (h, z + 1 - 2 * (z % 2))).astype(F32)

    hidden = gate_weight.shape[1]

    def out_term(first, ready):
        return out_products(out_cols, (after(act1, ready), act1_other, act0, act0_other), block, first, 2)

    def down_move(term, dz, *ready):
        return dp_move(after(term.astype(BF), *ready), lambda h, z: (h, z + dz)).astype(F32)

    d_act0_other = after(d_act0_other, term2)
    down13 = out_term(0, d_act0_other)
    one, three = down_move(down13[0], 1), down_move(down13[1], 3)
    far = in_term(3, 1, BF, down13)[0]
    far_sum = over_y(far)
    down20 = out_term(2, far)
    two = down_move(down20[0], 2, one, three)
    core2 = scatter_core(after(term2, far))
    near = in_term(1, 2, F32, down20, one, three, core2)
    in_z, in_y = near[0], near[1]
    far_n0 = scatter_far(core2)
    near_m1 = scatter_near(after(far_m1, near))
    own = in_term(0, 1, F32, far_sum, two, far_n0)[0]
    total2 = scatter_near(after(far_n0, far_sum))
    from_y = over_y(after(in_y.astype(BF), far_sum))
    from_z = over_link((in_z + far_sum).astype(BF))
    m1 = scatter_pair(after(near_m1, own))
    down_grads = down20[1] + one + two + three
    in_grads = own + from_y + from_z
    input_grads = r1 + norm_back(x0, inv0, scatter_pair(after(total2, far_sum)), norm_gain)
    final_states = (h1.astype(F32) + m1).astype(BF)
    return (final_states, input_grads, in_grads[:, :hidden], in_grads[:, hidden:], down_grads)


def solution(mesh):
    in_specs = (
        P(("section", "dp"), None),
        P(),
        P(None, "section"),
        P(None, "section"),
        P("section", None),
        P(("section", "dp"), None),
    )
    out_specs = (
        P(("section", "dp"), None),
        P(("section", "dp"), None),
        P("dp", "section"),
        P("dp", "section"),
        P("section", "dp"),
    )
    return jax.shard_map(local, mesh=mesh, in_specs=in_specs, out_specs=out_specs, check_vma=False)
```

```python
import jax
import jax.numpy as jnp
from jax import lax
from jax.experimental import pallas as pl
from jax.experimental.pallas import tpu as pltpu
from jax.sharding import PartitionSpec as P

EPS = 1e-06
N_Y, N_X, N_C = 2, 4, 2
N_H, N_Z = 2, 4
BF = jnp.bfloat16
F32 = jnp.float32


def section_move(values, dy, dx, dc):
    pairs = []
    for y in range(N_Y):
        for x in range(N_X):
            for c in range(N_C):
                source = (y * N_X + x) * N_C + c
                target = ((y + dy) % N_Y * N_X + (x + dx) % N_X) * N_C + (c + dc) % N_C
                pairs.append((source, target))
    return lax.ppermute(values, "section", pairs)


def dp_move(values, target):
    pairs = []
    for h in range(N_H):
        for z in range(N_Z):
            to_h, to_z = target(h, z)
            pairs.append((h * N_Z + z, to_h % N_H * N_Z + to_z % N_Z))
    return lax.ppermute(values, "dp", pairs)


def over_h(values):
    return dp_move(values, lambda h, z: (h + 1, z))


def over_z(values):
    return dp_move(values, lambda h, z: (h, z + 2))


def after(values, *others):
    return lax.optimization_barrier((values,) + others)[0]


def stacked(parts):
    return lax.optimization_barrier(jnp.concatenate(parts, axis=0))


def gather_line(pair, *ready):
    first, second, third = (section_move(pair, 0, -dx, 0) for dx in range(N_X)[1:])
    first = after(first, *ready)
    return stacked([pair, first, after(second, first), after(third, first)])


def gather_near(pair):
    return stacked([pair, section_move(pair, 0, -1, 0)])


def gather_far(near):
    return stacked([near, section_move(near, 0, -2, 0)])


def gather_core(line):
    return stacked([line, section_move(line, 0, 0, 1)])


def gather_pair(own):
    return stacked([own, section_move(own, 1, 0, 0)])


def scatter_core(terms):
    half = terms.shape[0] // N_C
    return terms[:half].astype(F32) + section_move(terms[half:], 0, 0, 1).astype(F32)


def scatter_line(line, *ready):
    line_low = line.astype(BF)
    quarter = line.shape[0] // N_X
    first, second, third = (
        section_move(line_low[dx * quarter : (dx + 1) * quarter], 0, dx, 0).astype(F32)
        for dx in range(N_X)[1:]
    )
    total = after(line[:quarter] + first, *ready)
    return total + after(second, total) + after(third, total)


def scatter_far(line):
    half = line.shape[0] // 2
    return line[:half] + section_move(line[half:].astype(BF), 0, 2, 0).astype(F32)


def scatter_near(line):
    quarter = line.shape[0] // 2
    return line[:quarter] + section_move(line[quarter:].astype(BF), 0, 1, 0).astype(F32)


def scatter_pair(total):
    own = total.shape[0] // N_Y
    return total[:own] + section_move(total[own:].astype(BF), 1, 0, 0).astype(F32)


def normalize(values):
    widened = values.astype(F32)
    inv_rms = lax.rsqrt(jnp.mean(widened * widened, axis=-1, keepdims=True) + EPS)
    return (widened * inv_rms, inv_rms)


def norm_back(x_hat, inv_rms, d_normed, norm_gain):
    scaled = d_normed * norm_gain
    return inv_rms * (scaled - x_hat * jnp.mean(scaled * x_hat, axis=-1, keepdims=True))


def dot(left, right):
    return jnp.dot(left, right, preferred_element_type=F32)


def dot_t(left, right):
    return lax.dot_general(left, right, (((1,), (1,)), ((), ())), preferred_element_type=F32)


def dot_tokens(left, right):
    return lax.dot_general(left, right, (((0,), (0,)), ((), ())), preferred_element_type=F32)


def in_kernel(*refs):
    cols, (d_other, gate_other, up_other), rows = refs[:4], refs[4:7], (refs[7:10], refs[10:13])
    out, grads = refs[13:]
    hidden = d_other.shape[1]
    parts = (pl.ds(0, hidden), pl.ds(hidden, hidden))

    @pl.when(pl.program_id(0) == 0)
    def _():
        d_wide = d_other[...].astype(F32)
        for part, factor in zip(parts, (gate_other, up_other)):
            grads[:, part] = (d_wide * factor[...].astype(F32)).astype(BF)

    for part, own in zip(parts, rows):
        total = dot_tokens(cols[0][...], own[0][...])
        for col, row in zip(cols[1:], own[1:]):
            total = total + dot_tokens(col[...], row[...])
        out[0, :, part] = (total + dot_tokens(cols[3][...], grads[:, part])).astype(out.dtype)


def column_specs(cols, block, first):
    return [pl.BlockSpec((c.shape[0], block), lambda i: (0, first + i)) for c in cols]


def row_specs(rows, hidden):
    return [pl.BlockSpec((r.shape[0], hidden), lambda i, part=part: (0, part)) for r, part in rows]


def in_products(cols, factors, gate_rows, up_rows, block, first, count, dtype):
    tokens, hidden = factors[0][0].shape
    rows = factors + gate_rows + up_rows
    return pl.pallas_call(
        in_kernel,
        grid=(count,),
        in_specs=column_specs(cols, block, first) + row_specs(rows, hidden),
        out_specs=pl.BlockSpec((1, block, 2 * hidden), lambda i: (i, 0, 0)),
        out_shape=jax.ShapeDtypeStruct((count, block, 2 * hidden), dtype),
        scratch_shapes=[pltpu.VMEM((tokens, 2 * hidden), BF)],
        compiler_params=pltpu.CompilerParams(vmem_limit_bytes=36 * 1024 * 1024),
        cost_estimate=pl.CostEstimate(
            flops=16 * count * tokens * block * hidden,
            bytes_accessed=18 * tokens * hidden + 8 * count * block * hidden,
            transcendentals=0,
        ),
    )(*cols, *(r for r, _ in rows))


def out_kernel(*refs):
    cols, rows, out = refs[:4], refs[4:8], refs[8]
    total = dot_tokens(rows[0][...], cols[0][...])
    for row, col in zip(rows[1:], cols[1:]):
        total = total + dot_tokens(row[...], col[...])
    out[0] = total


def out_products(cols, rows, block, first, count):
    tokens, hidden = rows[0].shape
    return pl.pallas_call(
        out_kernel,
        grid=(count,),
        in_specs=column_specs(cols, block, first) + row_specs([(r, 0) for r in rows], hidden),
        out_specs=pl.BlockSpec((1, hidden, block), lambda i: (i, 0, 0)),
        out_shape=jax.ShapeDtypeStruct((count, hidden, block), F32),
        compiler_params=pltpu.CompilerParams(vmem_limit_bytes=36 * 1024 * 1024),
        cost_estimate=pl.CostEstimate(
            flops=8 * count * tokens * block * hidden,
            bytes_accessed=16 * tokens * hidden + 4 * count * block * hidden,
            transcendentals=0,
        ),
    )(*cols, *rows)


def local(states, norm_gain, gate_weight, up_weight, down_weight, cotangent):
    width = states.shape[1]
    block = width // (N_H * N_Z)
    me = lax.axis_index("dp")
    my_h, my_z = me // N_Z, me % N_Z
    side = my_z // 2

    def columns(values, numbers):
        parts = [lax.dynamic_slice_in_dim(values, n * block, block, axis=1) for n in numbers]
        return jnp.concatenate(parts, axis=1)

    def of_h(values, h):
        return columns(values, [h * N_Z + (my_z + dz) % N_Z for dz in (1, 3, 2, 0)])

    def of_side(values, s):
        return columns(
            values,
            [
                (my_h + dh) % N_H * N_Z + s * 2 + (my_z + dz) % 2
                for dh in range(N_H)
                for dz in range(2)
            ],
        )

    def project(normed):
        gate_pre = dot(normed, gate_weight)
        up_pre = dot(normed, up_weight)
        sig = jax.nn.sigmoid(gate_pre)
        act = (gate_pre * sig * up_pre).astype(BF)
        to_gate = up_pre * sig * (1.0 + gate_pre * (1.0 - sig))
        to_up = gate_pre * sig
        return act, to_gate, to_up

    x0, inv0 = normalize(states)
    pair0 = gather_pair((x0 * norm_gain).astype(BF))
    line0 = gather_line(pair0)
    cot_pair = gather_pair(after(cotangent, pair0))
    normed0 = gather_core(after(line0, cot_pair))
    cot_near = gather_near(after(cot_pair, line0))
    act0, to_gate0, to_up0 = project(normed0)
    both0 = jnp.concatenate([to_gate0.astype(BF), to_up0.astype(BF)], axis=1)
    core0 = scatter_core(dot(act0, down_weight).astype(BF))
    normed0_half = over_z(after(of_side(line0, 1 - side), core0))
    total0 = scatter_line(core0, normed0_half, cot_near)
    cot_line = gather_far(after(cot_near, total0))
    both0_other = over_z(after(both0, total0))
    h1 = (states.astype(F32) + scatter_pair(total0)).astype(BF)

    x1, inv1 = normalize(h1)
    pair1 = after(gather_pair((x1 * norm_gain).astype(BF)), cot_line)
    grad1_half = over_h(after(of_h(cot_line, 1 - my_h), pair1))
    line1 = gather_line(pair1, both0_other, grad1_half)
    grad1 = gather_core(after(cot_line, line1))
    normed1 = gather_core(line1)
    normed0_other = gather_core(after(normed0_half, normed1))
    act1, to_gate1, to_up1 = project(normed1)
    d_act1 = dot_t(grad1, down_weight)
    gate1 = (d_act1 * to_gate1).astype(BF)
    up1 = (d_act1 * to_up1).astype(BF)
    term1 = (dot_t(gate1, gate_weight) + dot_t(up1, up_weight)).astype(BF)
    core1 = scatter_core(term1)
    normed1_half = over_z(after(of_side(line1, 1 - side), term1))
    act0_other = over_h(after(act0, term1))
    term_m1 = dot(after(act1, core1), down_weight).astype(BF)
    total1 = scatter_line(core1, normed1_half, act0_other, term_m1)
    gate1_other = over_z(after(gate1, total1))
    core_m1 = scatter_core(after(term_m1, total1))
    r1 = cotangent.astype(F32) + norm_back(x1, inv1, scatter_pair(total1), norm_gain)
    pair2 = after(gather_pair(r1.astype(BF)), core_m1, gate1_other)
    up1_other = over_z(after(up1, gate1_other))
    act1_other = over_h(after(act1, pair2))
    grad1_other = gather_core(after(grad1_half, pair2))
    line2 = after(gather_line(pair2, up1_other, act1_other), grad1_other, normed0_other)
    grad0_half = over_h(of_h(line2, 1 - my_h))
    grad0 = gather_core(line2)

    d_act0 = dot_t(grad0, down_weight)
    d_act0_other = over_z(d_act0.astype(BF))
    normed1_other = gather_core(after(normed1_half, d_act0))
    gate0 = (d_act0 * to_gate0).astype(BF)
    up0 = (d_act0 * to_up0).astype(BF)
    term2 = (dot_t(gate0, gate_weight) + dot_t(up0, up_weight)).astype(BF)
    grad0_other = gather_core(after(grad0_half, term2))
    far_m1 = scatter_far(after(core_m1, term2))

    normed1_own, normed0_own = of_side(normed1, side), of_side(normed0, side)
    grad1_own, grad0_own = of_h(grad1, my_h), of_h(grad0, my_h)
    out_cols = (grad1_own, grad1_other, grad0_own, grad0_other)
    in_cols = (normed1_own, normed1_other, normed0_own, normed0_other)

    def in_term(first, count, dtype, *ready):
        factors = ((after(d_act0_other, term2, *ready), 0), (both0_other, 0), (both0_other, 1))
        gate_rows = ((gate1, 0), (gate1_other, 0), (gate0, 0))
        up_rows = ((up1, 0), (up1_other, 0), (up0, 0))
        return in_products(in_cols, factors, gate_rows, up_rows, block, first, count, dtype)

    def over_y(values):
        return dp_move(values, lambda h, z: (h + 1, z)).astype(F32)

    def over_link(values):
        return dp_move(values, lambda h, z: (h, z + 1 - 2 * (z % 2))).astype(F32)

    hidden = gate_weight.shape[1]

    def out_term(first, ready):
        return out_products(out_cols, (after(act1, ready), act1_other, act0, act0_other), block, first, 2)

    def down_move(term, dz, *ready):
        return dp_move(after(term.astype(BF), *ready), lambda h, z: (h, z + dz)).astype(F32)

    d_act0_other = after(d_act0_other, term2)
    down13 = out_term(0, d_act0_other)
    one, three = down_move(down13[0], 1), down_move(down13[1], 3)
    far = in_term(3, 1, BF, down13)[0]
    far_sum = over_y(far)
    down20 = out_term(2, far)
    two = down_move(down20[0], 2, one, three)
    core2 = scatter_core(after(term2, far))
    near = in_term(1, 2, F32, down20, one, three, core2)
    in_z, in_y = near[0], near[1]
    far_n0 = scatter_far(core2)
    near_m1 = scatter_near(after(far_m1, near))
    own = in_term(0, 1, F32, far_sum, two, far_n0)[0]
    total2 = scatter_near(after(far_n0, far_sum))
    from_y = over_y(after(in_y.astype(BF), far_sum))
    from_z = over_link((in_z + far_sum).astype(BF))
    m1 = scatter_pair(after(near_m1, own))
    down_grads = down20[1] + one + two + three
    in_grads = own + from_y + from_z
    input_grads = r1 + norm_back(x0, inv0, scatter_pair(after(total2, far_sum)), norm_gain)
    final_states = (h1.astype(F32) + m1).astype(BF)
    return (final_states, input_grads, in_grads[:, :hidden], in_grads[:, hidden:], down_grads)


def solution(mesh):
    in_specs = (
        P(("section", "dp"), None),
        P(),
        P(None, "section"),
        P(None, "section"),
        P("section", None),
        P(("section", "dp"), None),
    )
    out_specs = (
        P(("section", "dp"), None),
        P(("section", "dp"), None),
        P("dp", "section"),
        P("dp", "section"),
        P("section", "dp"),
    )
    return jax.shard_map(local, mesh=mesh, in_specs=in_specs, out_specs=out_specs, check_vma=False)
```
